32 devices in a mesh: row: 16 (over z, y, core), col: 2 (over x).
Axes of the slice: x: 2, y: 2, z: 4, core: 2. Of those that a mesh axis runs over, the one named last changes fastest.
Arguments:
- crop: bfloat16 [256, 256, 512], P('row', 'col'), may hold values from -6 to 6
- tissue: int32 [16, 16], P('row', 'col'), may hold values 0 or 1
- w_qkv: bfloat16 [512, 1536], replicated, may hold values from -0.25 to 0.25
- w_proj: bfloat16 [512, 512], replicated, may hold values from -0.25 to 0.25
- w_fc1: bfloat16 [512, 2048], replicated, may hold values from -0.25 to 0.25
- w_fc2: bfloat16 [2048, 512], replicated, may hold values from -0.125 to 0.125
- logit_scale: float32 [16], replicated, may hold values from 1.5 to 5.5
- bias_table: float32 [16, 31, 31], replicated, may hold values from 0 to 16
- norm1_gain: float32 [512], replicated, may hold values from 0.5 to 1.5
- norm1_bias: float32 [512], replicated, may hold values from -1 to 1
- norm2_gain: float32 [512], replicated, may hold values from 0.5 to 1.5
- norm2_bias: float32 [512], replicated, may hold values from -1 to 1
Outputs:
- block_out: bfloat16 [256, 256, 512], P('row', 'col')
The draws below stay inside these ranges and needn't reach their ends.
All inputs are finite; a program needn't handle non-finite values. No bound on the sum of `tissue` on one device may be relied on, other than what follows from the above.
Results may differ from the reference program's by a relative error of at most 0.012.
The reference program's roundings to bfloat16 on the way count: a program that leaves them out, or rounds other values in their place, can miss the bound.
Values may be sent and summed in bfloat16 or wider, within the bound.
A program may use at most 192 MiB of HBM per device.

```python
import math
import jax
import jax.numpy as jnp
import numpy as np
from jax import lax

DIM = 512
HEADS = 16
WIN = 16
HIDDEN_SIZE = 2048
HEAD_DIM = 32
SHIFT = 8
ROWS = 256
COLS = 256
WROWS = 16
WCOLS = 16


def plant(array, rng, smallest, high):
    shape = array.shape
    spot = [jax.random.randint(jax.random.fold_in(rng, axis), (), 0, shape[axis]) for axis in range(len(shape))]
    array = array.at[tuple(spot)].set(smallest)
    longest = shape.index(max(shape))
    spot[longest] = (spot[longest] + 1) % shape[longest]
    return array.at[tuple(spot)].set(high)


def block_levels(key, dims, pieces, least, largest):
    def one(axis_at, shards_of):
        steps = jax.random.uniform(jax.random.fold_in(jax.random.fold_in(key, 6), axis_at), (shards_of,), jnp.float32, least / len(pieces), largest / len(pieces))
        return jnp.repeat(jnp.exp(steps), dims[axis_at] // shards_of).reshape((-1,) + (1,) * (len(dims) - axis_at - 1))

    level = one(*pieces[0])
    for cut in pieces[1:]:
        level = level * one(*cut)
    return level


def scatter_about(stream_key, extent, scale, most, pieces=(), kind=jnp.bfloat16):
    array = scale * jax.random.normal(stream_key, extent, jnp.float32)
    if pieces:
        array = array * block_levels(stream_key, extent, pieces, -0.22, 0.18)
    return jnp.clip(array, -most, most).astype(kind)


def setup_inputs(seed: int = 0) -> dict:
    key_of = jax.random.split(jax.random.key(seed), 13)
    return {
        "crop": scatter_about(key_of[0], (ROWS, COLS, DIM), 1.0, 6.0, ((0, 16), (1, 2))),
        "tissue": plant((jax.random.randint(key_of[1], (WROWS, WCOLS), 0, 4) < 3).astype(jnp.int32), jax.random.fold_in(key_of[1], 1), 0, 1),
        "w_qkv": scatter_about(key_of[2], (DIM, 3 * DIM), DIM ** -0.5, 0.25),
        "w_proj": scatter_about(key_of[3], (DIM, DIM), DIM ** -0.5, 0.25),
        "w_fc1": scatter_about(key_of[4], (DIM, HIDDEN_SIZE), DIM ** -0.5, 0.25),
        "w_fc2": scatter_about(key_of[5], (HIDDEN_SIZE, DIM), HIDDEN_SIZE ** -0.5, 0.125),
        "logit_scale": jnp.clip(jax.random.uniform(key_of[6], (HEADS,), jnp.float32, 1.5, 5.5), 1.5, 5.5),
        "bias_table": jnp.clip(jax.random.uniform(key_of[7], (HEADS, 2 * WIN - 1, 2 * WIN - 1), jnp.float32, 0.0, 16.0), 0.0, 16.0),
        "norm1_gain": jnp.clip(1.0 + 0.1 * jax.random.normal(key_of[8], (DIM,), jnp.float32), 0.5, 1.5),
        "norm1_bias": scatter_about(key_of[9], (DIM,), 0.2, 1.0, (), jnp.float32),
        "norm2_gain": jnp.clip(1.0 + 0.1 * jax.random.normal(key_of[10], (DIM,), jnp.float32), 0.5, 1.5),
        "norm2_bias": scatter_about(key_of[11], (DIM,), 0.2, 1.0, (), jnp.float32),
    }


def offset_tables():
    places = np.arange(WIN * WIN)
    place_row = places // WIN
    place_col = places % WIN
    delta_row = place_row[:, None] - place_row[None, :] + WIN - 1
    delta_col = place_col[:, None] - place_col[None, :] + WIN - 1
    return (delta_row, delta_col)

def full_bias(bias_table):
    delta_row, delta_col = offset_tables()
    return bias_table[:, delta_row, delta_col]

def region_label(coords, total):
    return jnp.where(coords < total - WIN, 0, jnp.where(coords < total - SHIFT, 1, 2)).astype(jnp.int32)

def layer_norm(values, gain, offset):
    centre = lax.optimization_barrier(jnp.mean(values, axis=-1, keepdims=True))
    centred = values - centre
    spread = lax.optimization_barrier(jnp.mean(centred * centred, axis=-1, keepdims=True))
    return centred * lax.rsqrt(spread + 1e-05) * gain + offset

def unit_rows(values):
    return values * lax.rsqrt(lax.optimization_barrier(jnp.sum(values * values, axis=-1, keepdims=True)) + 1e-06)

def attend_windows(tokens, labels, token_mask, w_qkv, w_proj, head_scale, bias, norm1_gain, norm1_bias):
    count = tokens.shape[0]
    flat = tokens.reshape(count * WIN * WIN, DIM)
    triple = jnp.dot(flat, w_qkv, preferred_element_type=jnp.float32).astype(jnp.bfloat16)
    triple = triple.reshape(count, WIN * WIN, 3, HEADS, HEAD_DIM)
    query_unit = unit_rows(triple[:, :, 0].astype(jnp.float32)).astype(jnp.bfloat16)
    key_unit = unit_rows(triple[:, :, 1].astype(jnp.float32)).astype(jnp.bfloat16)
    values = triple[:, :, 2]
    scores = jnp.einsum('nqhd,nkhd->nhqk', query_unit.astype(jnp.float32), key_unit.astype(jnp.float32))
    same = labels[:, :, None] == labels[:, None, :]
    penalty = jnp.where(same, jnp.float32(0.0), jnp.float32(-100.0))
    scores = scores * head_scale[None, :, None, None] + bias[None] + penalty[:, None]
    highest = lax.optimization_barrier(jnp.max(scores, axis=-1, keepdims=True))
    raised = jnp.exp(scores - highest)
    weights = (raised / lax.optimization_barrier(jnp.sum(raised, axis=-1, keepdims=True))).astype(jnp.bfloat16)
    mixed = jnp.einsum('nhqk,nkhd->nqhd', weights.astype(jnp.float32), values.astype(jnp.float32)).astype(jnp.bfloat16)
    projected = jnp.dot(mixed.reshape(count * WIN * WIN, DIM), w_proj, preferred_element_type=jnp.float32)
    branch = layer_norm(projected, norm1_gain, norm1_bias)
    result = flat.astype(jnp.float32) + token_mask.reshape(-1, 1) * branch
    return result.astype(jnp.bfloat16).reshape(count, WIN * WIN, DIM)

def feed_forward(tokens, token_mask, w_fc1, w_fc2, norm2_gain, norm2_bias):
    hidden = jax.nn.gelu(jnp.dot(tokens, w_fc1, preferred_element_type=jnp.float32), approximate=False).astype(jnp.bfloat16)
    grown = jnp.dot(hidden, w_fc2, preferred_element_type=jnp.float32)
    return (tokens.astype(jnp.float32) + token_mask[:, None] * layer_norm(grown, norm2_gain, norm2_bias)).astype(jnp.bfloat16)

def reference(crop, tissue, w_qkv, w_proj, w_fc1, w_fc2, logit_scale, bias_table, norm1_gain, norm1_bias, norm2_gain, norm2_bias):
    rolled = jnp.roll(crop, (-SHIFT, -SHIFT), axis=(0, 1))
    windows = rolled.reshape(WROWS, WIN, WCOLS, WIN, DIM).transpose(0, 2, 1, 3, 4).reshape(WROWS, WCOLS, WIN * WIN, DIM)
    head_scale = jnp.exp(jnp.minimum(logit_scale, math.log(100.0)))
    bias = full_bias(bias_table)
    col_label = region_label(jnp.arange(COLS), COLS).reshape(WCOLS, WIN)

    def one_row(index):
        row_label = region_label(index * WIN + jnp.arange(WIN), ROWS)
        labels = (3 * row_label[None, :, None] + col_label[:, None, :]).reshape(WCOLS, WIN * WIN)
        flags = tissue[index].astype(jnp.float32)
        token_mask = jnp.broadcast_to(flags[:, None], (WCOLS, WIN * WIN))
        mixed = attend_windows(windows[index], labels, token_mask, w_qkv, w_proj, head_scale, bias, norm1_gain, norm1_bias)
        done = feed_forward(mixed.reshape(WCOLS * WIN * WIN, DIM), token_mask.reshape(-1), w_fc1, w_fc2, norm2_gain, norm2_bias)
        return done.reshape(WCOLS, WIN * WIN, DIM)
    finished = lax.map(one_row, jnp.arange(WROWS))
    finished = finished.reshape(WROWS, WCOLS, WIN, WIN, DIM).transpose(0, 2, 1, 3, 4).reshape(ROWS, COLS, DIM)
    return jnp.roll(finished, (SHIFT, SHIFT), axis=(0, 1))
```

```python
import math

import jax
import jax.numpy as jnp
from jax import lax
from jax.experimental import pallas as pl
from jax.experimental.pallas import tpu as pltpu
from jax.sharding import PartitionSpec as P

DIM = 512
HEADS = 16
WIN = 16
HEAD_DIM = 32
SHIFT = 8
TOKENS = WIN * WIN
SPAN = 2 * WIN * WIN
LOG2E = math.log2(math.e)


def shifted(x, axis, by):
    count = lax.axis_size(axis)
    return lax.ppermute(x, axis, [(i, (i + by) % count) for i in range(count)])


def nt_dot(a, b):
    return lax.dot_general(a, b, (((1,), (1,)), ((), ())), preferred_element_type=jnp.float32)


def tn_dot(a, b):
    return lax.dot_general(a, b, (((0,), (0,)), ((), ())), preferred_element_type=jnp.float32)


def nn_dot(a, b):
    return lax.dot_general(a, b, (((1,), (0,)), ((), ())), preferred_element_type=jnp.float32)


def half_of(axis):
    key = lax.broadcasted_iota(jnp.int32, (TOKENS, TOKENS), 0)
    query = lax.broadcasted_iota(jnp.int32, (TOKENS, TOKENS), 1)
    if axis == 0:
        key, query = key // WIN, query // WIN
    else:
        key, query = key % WIN, query % WIN
    return (key < SHIFT) != (query < SHIFT)


def bias_kernel(edge_ref, low_ref, high_ref, bias_ref, rows_ref, pen_ref):
    low = low_ref[...]
    high = high_ref[...]
    place = lax.broadcasted_iota(jnp.int32, (HEADS, SPAN), 1) % WIN
    for y in range(WIN):
        s = WIN - 1 - y
        first = pltpu.roll(low, (SPAN - s) % SPAN, 1)
        second = pltpu.roll(high, WIN - s, 1)
        rows_ref[:, y, :] = jnp.where(place < WIN - s, first, second)
    by_row = half_of(0) & (edge_ref[0] == 1)
    by_col = half_of(1) & (edge_ref[1] == 1)
    row_pen = jnp.where(by_row, jnp.float32(-100.0 * LOG2E), jnp.float32(0.0))
    pen_ref[0] = row_pen
    pen_ref[1] = jnp.where(by_col, jnp.float32(-100.0 * LOG2E), row_pen)

    def one_head(h, carry):
        rows = rows_ref[h]
        for v in range(WIN):
            lanes = WIN * (WIN - 1 - v)
            moved = pltpu.roll(rows, (SPAN - lanes) % SPAN, 1)[:, :TOKENS]
            at = slice(v * WIN, (v + 1) * WIN)
            bias_ref[0, h, at, :] = moved + pen_ref[0, at, :]
            bias_ref[1, h, at, :] = moved + pen_ref[1, at, :]
        return carry

    lax.fori_loop(0, HEADS, one_head, 0)


def build_bias(edges, bias_table):
    table = jnp.pad(bias_table * jnp.float32(LOG2E), ((0, 0), (0, 1), (0, 1)))
    low = table[:, :, :WIN].reshape(HEADS, SPAN)
    high = table[:, :, WIN:].reshape(HEADS, SPAN)
    return pl.pallas_call(
        bias_kernel,
        out_shape=jax.ShapeDtypeStruct((2, HEADS, TOKENS, TOKENS), jnp.float32),
        in_specs=[
            pl.BlockSpec(memory_space=pltpu.SMEM),
            pl.BlockSpec(memory_space=pltpu.VMEM),
            pl.BlockSpec(memory_space=pltpu.VMEM),
        ],
        out_specs=pl.BlockSpec(memory_space=pltpu.VMEM),
        scratch_shapes=[
            pltpu.VMEM((HEADS, WIN, SPAN), jnp.float32),
            pltpu.VMEM((2, TOKENS, TOKENS), jnp.float32),
        ],
        compiler_params=pltpu.CompilerParams(vmem_limit_bytes=24 * 2**20),
        cost_estimate=pl.CostEstimate(
            flops=4 * 2**20, bytes_accessed=20 * 2**20, transcendentals=0
        ),
        name="bias",
    )(edges, low, high)


def layer_norm(values, gain, offset):
    centre = jnp.mean(values, axis=-1, keepdims=True)
    centred = values - centre
    spread = jnp.mean(centred * centred, axis=-1, keepdims=True)
    return centred * lax.rsqrt(spread + 1e-05) * gain + offset


def gelu(x):
    return 0.5 * x * (1.0 + lax.erf(x * jnp.float32(math.sqrt(0.5))))


def window_kernel(
    tissue_ref,
    scale_ref,
    x_ref,
    wqkv_ref,
    wproj_ref,
    wfc1_ref,
    wfc2_ref,
    bias_ref,
    norm_ref,
    out_ref,
    triple_ref,
    mixed_ref,
):
    w = pl.program_id(0)
    x = x_ref[...].reshape(TOKENS, DIM)
    triple = nt_dot(wqkv_ref[...], x).astype(jnp.bfloat16)
    for at in range(2):
        part = triple[at * DIM : (at + 1) * DIM].astype(jnp.float32)
        part = part.reshape(HEADS, HEAD_DIM, TOKENS)
        part = part * lax.rsqrt(jnp.sum(part * part, axis=1, keepdims=True) + 1e-06)
        triple_ref[at * DIM : (at + 1) * DIM, :] = part.reshape(DIM, TOKENS).astype(jnp.bfloat16)
    triple_ref[2 * DIM :, :] = triple[2 * DIM :]
    ones = jnp.ones((16, TOKENS), jnp.bfloat16)
    for h in range(HEADS):
        at = h * HEAD_DIM
        query = triple_ref[at : at + HEAD_DIM, :]
        key = triple_ref[DIM + at : DIM + at + HEAD_DIM, :]
        value = triple_ref[2 * DIM + at : 2 * DIM + at + HEAD_DIM, :]
        scores = tn_dot(key, query) * scale_ref[h] + bias_ref[0, h]
        highest = jnp.max(scores, axis=0, keepdims=True)
        raised = jnp.exp2(scores - highest).astype(jnp.bfloat16)
        both = nn_dot(jnp.concatenate([value, ones], axis=0), raised)
        mixed = both[:HEAD_DIM] * (1.0 / both[HEAD_DIM : HEAD_DIM + 1])
        mixed_ref[at : at + HEAD_DIM, :] = mixed.astype(jnp.bfloat16)
    keep = tissue_ref[0, w].astype(jnp.float32)
    projected = tn_dot(mixed_ref[...], wproj_ref[...])
    branch = layer_norm(projected, norm_ref[0:1, :], norm_ref[1:2, :])
    after = (x.astype(jnp.float32) + keep * branch).astype(jnp.bfloat16)
    hidden = gelu(nn_dot(after, wfc1_ref[...])).astype(jnp.bfloat16)
    grown = nn_dot(hidden, wfc2_ref[...])
    branch = layer_norm(grown, norm_ref[2:3, :], norm_ref[3:4, :])
    final = (after.astype(jnp.float32) + keep * branch).astype(jnp.bfloat16)
    out_ref[...] = final.reshape(WIN, WIN, DIM)


def run_windows(tissue, scale, rolled, weights, bias, norms):
    cols = rolled.shape[1]
    count = cols // WIN
    smem = pl.BlockSpec(memory_space=pltpu.SMEM)
    whole = pl.BlockSpec(memory_space=pltpu.VMEM)
    tile = pl.BlockSpec((WIN, WIN, DIM), lambda w: (0, w, 0))
    table = pl.BlockSpec(
        (1, HEADS, TOKENS, TOKENS), lambda w: (jnp.where(w == count - 1, 1, 0), 0, 0, 0)
    )
    return pl.pallas_call(
        window_kernel,
        grid=(count,),
        out_shape=jax.ShapeDtypeStruct(rolled.shape, jnp.bfloat16),
        in_specs=[smem, smem, tile] + [whole] * 4 + [table, whole],
        out_specs=tile,
        scratch_shapes=[
            pltpu.VMEM((3 * DIM, TOKENS), jnp.bfloat16),
            pltpu.VMEM((DIM, TOKENS), jnp.bfloat16),
        ],
        compiler_params=pltpu.CompilerParams(
            vmem_limit_bytes=48 * 2**20, dimension_semantics=("arbitrary",)
        ),
        cost_estimate=pl.CostEstimate(
            flops=count * 2 * 10**9, bytes_accessed=16 * 2**20, transcendentals=count * 2**20
        ),
        name="windows",
    )(tissue, scale, rolled, *weights, bias, norms)


def on_device(
    crop,
    tissue,
    w_qkv,
    w_proj,
    w_fc1,
    w_fc2,
    logit_scale,
    bias_table,
    norm1_gain,
    norm1_bias,
    norm2_gain,
    norm2_bias,
):
    tile_rows, tile_cols = (crop.shape[0], crop.shape[1])
    edges = jnp.stack(
        [
            (lax.axis_index("row") == lax.axis_size("row") - 1).astype(jnp.int32),
            (lax.axis_index("col") == lax.axis_size("col") - 1).astype(jnp.int32),
        ]
    )
    scale = jnp.exp(jnp.minimum(logit_scale, math.log(100.0))) * jnp.float32(LOG2E)
    weights = (w_qkv.T, w_proj, w_fc1, w_fc2)
    norms = jnp.stack([norm1_gain, norm1_bias, norm2_gain, norm2_bias])
    bias = build_bias(edges, bias_table)
    beside = shifted(crop[:, :SHIFT], "col", -1)
    widened = jnp.concatenate([crop[:, SHIFT:], beside], axis=1)
    below = shifted(widened[:SHIFT], "row", -1)
    rolled = jnp.concatenate([widened[SHIFT:], below], axis=0)
    finished = run_windows(tissue, scale, rolled, weights, bias, norms)
    above = shifted(finished[tile_rows - SHIFT :], "row", 1)
    lifted = jnp.concatenate([above, finished[: tile_rows - SHIFT]], axis=0)
    leftward = shifted(lifted[:, tile_cols - SHIFT :], "col", 1)
    return jnp.concatenate([leftward, lifted[:, : tile_cols - SHIFT]], axis=1)


def solution(mesh):
    in_specs = (P("row", "col", None), P("row", "col")) + (P(),) * 10
    return jax.shard_map(
        on_device,
        mesh=mesh,
        in_specs=in_specs,
        out_specs=P("row", "col", None),
        check_vma=False,
    )
```

```python
import functools
import math

import jax
import jax.numpy as jnp
from jax import lax
from jax.experimental import pallas as pl
from jax.experimental.pallas import tpu as pltpu
from jax.sharding import PartitionSpec as P

DIM = 512
HEADS = 16
WIN = 16
HEAD_DIM = 32
SHIFT = 8
TOKENS = WIN * WIN
SPAN = 2 * WIN * WIN
LOG2E = math.log2(math.e)


def shifted(x, axis, by):
    count = lax.axis_size(axis)
    return lax.ppermute(x, axis, [(i, (i + by) % count) for i in range(count)])


def shifted_both(x, by):
    rows, cols = (lax.axis_size("row"), lax.axis_size("col"))
    pairs = [
        (r * cols + c, (r + by) % rows * cols + (c + by) % cols)
        for r in range(rows)
        for c in range(cols)
    ]
    return lax.ppermute(x, ("row", "col"), pairs)


def nt_dot(a, b):
    return lax.dot_general(a, b, (((1,), (1,)), ((), ())), preferred_element_type=jnp.float32)


def tn_dot(a, b):
    return lax.dot_general(a, b, (((0,), (0,)), ((), ())), preferred_element_type=jnp.float32)


def nn_dot(a, b):
    return lax.dot_general(a, b, (((1,), (0,)), ((), ())), preferred_element_type=jnp.float32)


def half_of(axis):
    key = lax.broadcasted_iota(jnp.int32, (TOKENS, TOKENS), 0)
    query = lax.broadcasted_iota(jnp.int32, (TOKENS, TOKENS), 1)
    if axis == 0:
        key, query = key // WIN, query // WIN
    else:
        key, query = key % WIN, query % WIN
    return (key < SHIFT) != (query < SHIFT)


def bias_kernel(edge_ref, low_ref, high_ref, inner_ref, last_ref, rows_ref, pen_ref):
    low = low_ref[...]
    high = high_ref[...]
    place = lax.broadcasted_iota(jnp.int32, (HEADS, SPAN), 1) % WIN
    for y in range(WIN):
        s = WIN - 1 - y
        first = pltpu.roll(low, (SPAN - s) % SPAN, 1)
        second = pltpu.roll(high, WIN - s, 1)
        rows_ref[:, y, :] = jnp.where(place < WIN - s, first, second)
    by_row = half_of(0) & (edge_ref[0] == 1)
    by_col = half_of(1) & (edge_ref[1] == 1)
    row_pen = jnp.where(by_row, jnp.float32(-100.0 * LOG2E), jnp.float32(0.0))
    pen_ref[0] = row_pen
    pen_ref[1] = jnp.where(by_col, jnp.float32(-100.0 * LOG2E), row_pen)

    def one_head(h, carry):
        rows = rows_ref[h]
        for v in range(WIN):
            lanes = WIN * (WIN - 1 - v)
            moved = pltpu.roll(rows, (SPAN - lanes) % SPAN, 1)[:, :TOKENS]
            at = slice(v * WIN, (v + 1) * WIN)
            inner_ref[h, at, :] = moved + pen_ref[0, at, :]
            last_ref[h, at, :] = moved + pen_ref[1, at, :]
        return carry

    lax.fori_loop(0, HEADS, one_head, 0)


def build_bias(edges, bias_table):
    table = jnp.pad(bias_table * jnp.float32(LOG2E), ((0, 0), (0, 1), (0, 1)))
    low = table[:, :, :WIN].reshape(HEADS, SPAN)
    high = table[:, :, WIN:].reshape(HEADS, SPAN)
    return pl.pallas_call(
        bias_kernel,
        out_shape=[jax.ShapeDtypeStruct((HEADS, TOKENS, TOKENS), jnp.float32)] * 2,
        in_specs=[
            pl.BlockSpec(memory_space=pltpu.SMEM),
            pl.BlockSpec(memory_space=pltpu.VMEM),
            pl.BlockSpec(memory_space=pltpu.VMEM),
        ],
        out_specs=[pl.BlockSpec(memory_space=pltpu.VMEM)] * 2,
        scratch_shapes=[
            pltpu.VMEM((HEADS, WIN, SPAN), jnp.float32),
            pltpu.VMEM((2, TOKENS, TOKENS), jnp.float32),
        ],
        compiler_params=pltpu.CompilerParams(vmem_limit_bytes=24 * 2**20),
        cost_estimate=pl.CostEstimate(
            flops=4 * 2**20, bytes_accessed=20 * 2**20, transcendentals=0
        ),
        name="bias",
    )(edges, low, high)


def layer_norm(values, gain, offset):
    centre = jnp.mean(values, axis=-1, keepdims=True)
    centred = values - centre
    spread = jnp.mean(centred * centred, axis=-1, keepdims=True)
    return centred * lax.rsqrt(spread + 1e-05) * gain + offset


def gelu(x):
    return 0.5 * x * (1.0 + lax.erf(x * jnp.float32(math.sqrt(0.5))))


def window_kernel(
    first,
    tissue_ref,
    scale_ref,
    top_ref,
    bottom_ref,
    wqkv_ref,
    wproj_ref,
    wfc1_ref,
    wfc2_ref,
    norm_ref,
    bias_ref,
    top_out_ref,
    bottom_out_ref,
    triple_ref,
    mixed_ref,
):
    w = pl.program_id(0)
    half = SHIFT * WIN
    x = jnp.concatenate(
        [top_ref[...].reshape(half, DIM), bottom_ref[...].reshape(half, DIM)], axis=0
    )
    triple = nt_dot(wqkv_ref[...], x).astype(jnp.bfloat16)
    for at in range(2):
        part = triple[at * DIM : (at + 1) * DIM].astype(jnp.float32)
        part = part.reshape(HEADS, HEAD_DIM, TOKENS)
        part = part * lax.rsqrt(jnp.sum(part * part, axis=1, keepdims=True) + 1e-06)
        triple_ref[at * DIM : (at + 1) * DIM, :] = part.reshape(DIM, TOKENS).astype(jnp.bfloat16)
    triple_ref[2 * DIM :, :] = triple[2 * DIM :]
    ones = jnp.ones((16, TOKENS), jnp.bfloat16)
    for h in range(HEADS):
        at = h * HEAD_DIM
        query = triple_ref[at : at + HEAD_DIM, :]
        key = triple_ref[DIM + at : DIM + at + HEAD_DIM, :]
        value = triple_ref[2 * DIM + at : 2 * DIM + at + HEAD_DIM, :]
        scores = tn_dot(key, query) * scale_ref[h] + bias_ref[h]
        highest = jnp.max(scores, axis=0, keepdims=True)
        raised = jnp.exp2(scores - highest).astype(jnp.bfloat16)
        both = nn_dot(jnp.concatenate([value, ones], axis=0), raised)
        mixed = both[:HEAD_DIM] * (1.0 / both[HEAD_DIM : HEAD_DIM + 1])
        mixed_ref[at : at + HEAD_DIM, :] = mixed.astype(jnp.bfloat16)
    keep = tissue_ref[0, first + w].astype(jnp.float32)
    projected = tn_dot(mixed_ref[...], wproj_ref[...])
    branch = layer_norm(projected, norm_ref[0:1, :], norm_ref[1:2, :])
    after = (x.astype(jnp.float32) + keep * branch).astype(jnp.bfloat16)
    hidden = gelu(nn_dot(after, wfc1_ref[...])).astype(jnp.bfloat16)
    grown = nn_dot(hidden, wfc2_ref[...])
    branch = layer_norm(grown, norm_ref[2:3, :], norm_ref[3:4, :])
    final = (after.astype(jnp.float32) + keep * branch).astype(jnp.bfloat16)
    top_out_ref[...] = final[:half].reshape(SHIFT, WIN, DIM)
    bottom_out_ref[...] = final[half:].reshape(SHIFT, WIN, DIM)


def run_windows(first, tissue, scale, top, bottom, weights, norms, bias):
    count = top.shape[1] // WIN
    smem = pl.BlockSpec(memory_space=pltpu.SMEM)
    whole = pl.BlockSpec(memory_space=pltpu.VMEM)
    tile = pl.BlockSpec((SHIFT, WIN, DIM), lambda w: (0, w, 0))
    half = jax.ShapeDtypeStruct(top.shape, jnp.bfloat16)
    return pl.pallas_call(
        functools.partial(window_kernel, first),
        grid=(count,),
        out_shape=[half, half],
        in_specs=[smem, smem, tile, tile] + [whole] * 6,
        out_specs=[tile, tile],
        scratch_shapes=[
            pltpu.VMEM((3 * DIM, TOKENS), jnp.bfloat16),
            pltpu.VMEM((DIM, TOKENS), jnp.bfloat16),
        ],
        compiler_params=pltpu.CompilerParams(
            vmem_limit_bytes=32 * 2**20, dimension_semantics=("arbitrary",)
        ),
        cost_estimate=pl.CostEstimate(
            flops=count * 7 * 10**9, bytes_accessed=4 * 2**20, transcendentals=count * 2**20
        ),
        name="windows",
    )(tissue, scale, top, bottom, *weights, norms, bias)


def on_device(
    crop,
    tissue,
    w_qkv,
    w_proj,
    w_fc1,
    w_fc2,
    logit_scale,
    bias_table,
    norm1_gain,
    norm1_bias,
    norm2_gain,
    norm2_bias,
):
    tile_cols = crop.shape[1]
    edges = jnp.stack(
        [
            (lax.axis_index("row") == lax.axis_size("row") - 1).astype(jnp.int32),
            (lax.axis_index("col") == lax.axis_size("col") - 1).astype(jnp.int32),
        ]
    )
    scale = jnp.exp(jnp.minimum(logit_scale, math.log(100.0))) * jnp.float32(LOG2E)
    weights = (w_qkv.T, w_proj, w_fc1, w_fc2)
    norms = jnp.stack([norm1_gain, norm1_bias, norm2_gain, norm2_bias])
    inner_bias, last_bias = build_bias(edges, bias_table)
    windows = tile_cols // WIN
    bounds = [windows, windows - 1, windows * 5 // 8, windows // 4, 0]
    parts = [(lo, hi) for hi, lo in zip(bounds, bounds[1:]) if hi > lo]
    side = shifted(crop[SHIFT:, :SHIFT], "col", -1)
    corner = shifted_both(crop[:SHIFT, :SHIFT], -1)
    tops, bottoms = ([], [])
    for lo, hi in parts:
        start, stop = (lo * WIN + SHIFT, hi * WIN + SHIFT)
        top = crop[SHIFT:, start : min(stop, tile_cols)]
        bottom = shifted(crop[:SHIFT, start : min(stop, tile_cols)], "row", -1)
        if stop > tile_cols:
            top = jnp.concatenate([top, side], axis=1)
            bottom = jnp.concatenate([bottom, corner], axis=1)
        tops.append(top)
        bottoms.append(bottom)
    own, above = ([], [])
    for (lo, hi), top, bottom in zip(parts, tops, bottoms):
        bias = last_bias if hi == windows else inner_bias
        top, bottom = run_windows(lo, tissue, scale, top, bottom, weights, norms, bias)
        if hi == windows:
            from_left = shifted(top[:, -SHIFT:], "col", 1)
            from_corner = shifted_both(bottom[:, -SHIFT:], 1)
            top, bottom = (top[:, :-SHIFT], bottom[:, :-SHIFT])
        own.insert(0, top)
        above.insert(0, shifted(bottom, "row", 1))
    upper = jnp.concatenate([from_corner] + above, axis=1)
    lower = jnp.concatenate([from_left] + own, axis=1)
    return jnp.concatenate([upper, lower], axis=0)


def solution(mesh):
    in_specs = (P("row", "col", None), P("row", "col")) + (P(),) * 10
    return jax.shard_map(
        on_device,
        mesh=mesh,
        in_specs=in_specs,
        out_specs=P("row", "col", None),
        check_vma=False,
    )
```

```python
import functools
import math

import jax
import jax.numpy as jnp
from jax import lax
from jax.experimental import pallas as pl
from jax.experimental.pallas import tpu as pltpu
from jax.sharding import PartitionSpec as P

DIM = 512
HEADS = 16
WIN = 16
HEAD_DIM = 32
SHIFT = 8
TOKENS = WIN * WIN
SPAN = 2 * WIN * WIN
LOG2E = math.log2(math.e)


def shifted(x, axis, by):
    count = lax.axis_size(axis)
    return lax.ppermute(x, axis, [(i, (i + by) % count) for i in range(count)])


def shifted_both(x, by):
    rows, cols = (lax.axis_size("row"), lax.axis_size("col"))
    pairs = [
        (r * cols + c, (r + by) % rows * cols + (c + by) % cols)
        for r in range(rows)
        for c in range(cols)
    ]
    return lax.ppermute(x, ("row", "col"), pairs)


def nt_dot(a, b):
    return lax.dot_general(a, b, (((1,), (1,)), ((), ())), preferred_element_type=jnp.float32)


def tn_dot(a, b):
    return lax.dot_general(a, b, (((0,), (0,)), ((), ())), preferred_element_type=jnp.float32)


def nn_dot(a, b):
    return lax.dot_general(a, b, (((1,), (0,)), ((), ())), preferred_element_type=jnp.float32)


def half_of(axis):
    key = lax.broadcasted_iota(jnp.int32, (TOKENS, TOKENS), 0)
    query = lax.broadcasted_iota(jnp.int32, (TOKENS, TOKENS), 1)
    if axis == 0:
        key, query = key // WIN, query // WIN
    else:
        key, query = key % WIN, query % WIN
    return (key < SHIFT) != (query < SHIFT)


def bias_kernel(edge_ref, low_ref, high_ref, inner_ref, last_ref, rows_ref, pen_ref):
    low = low_ref[...]
    high = high_ref[...]
    place = lax.broadcasted_iota(jnp.int32, (HEADS, SPAN), 1) % WIN
    for y in range(WIN):
        s = WIN - 1 - y
        first = pltpu.roll(low, (SPAN - s) % SPAN, 1)
        second = pltpu.roll(high, WIN - s, 1)
        rows_ref[:, y, :] = jnp.where(place < WIN - s, first, second)
    by_row = half_of(0) & (edge_ref[0] == 1)
    by_col = half_of(1) & (edge_ref[1] == 1)
    row_pen = jnp.where(by_row, jnp.float32(-100.0 * LOG2E), jnp.float32(0.0))
    pen_ref[0] = row_pen
    pen_ref[1] = jnp.where(by_col, jnp.float32(-100.0 * LOG2E), row_pen)

    def one_head(h, carry):
        rows = rows_ref[h]
        for v in range(WIN):
            lanes = WIN * (WIN - 1 - v)
            moved = pltpu.roll(rows, (SPAN - lanes) % SPAN, 1)[:, :TOKENS]
            at = slice(v * WIN, (v + 1) * WIN)
            inner_ref[h, at, :] = moved + pen_ref[0, at, :]
            last_ref[h, at, :] = moved + pen_ref[1, at, :]
        return carry

    lax.fori_loop(0, HEADS, one_head, 0)


def build_bias(edges, bias_table):
    table = jnp.pad(bias_table * jnp.float32(LOG2E), ((0, 0), (0, 1), (0, 1)))
    low = table[:, :, :WIN].reshape(HEADS, SPAN)
    high = table[:, :, WIN:].reshape(HEADS, SPAN)
    return pl.pallas_call(
        bias_kernel,
        out_shape=[jax.ShapeDtypeStruct((HEADS, TOKENS, TOKENS), jnp.float32)] * 2,
        in_specs=[
            pl.BlockSpec(memory_space=pltpu.SMEM),
            pl.BlockSpec(memory_space=pltpu.VMEM),
            pl.BlockSpec(memory_space=pltpu.VMEM),
        ],
        out_specs=[pl.BlockSpec(memory_space=pltpu.VMEM)] * 2,
        scratch_shapes=[
            pltpu.VMEM((HEADS, WIN, SPAN), jnp.float32),
            pltpu.VMEM((2, TOKENS, TOKENS), jnp.float32),
        ],
        compiler_params=pltpu.CompilerParams(vmem_limit_bytes=24 * 2**20),
        cost_estimate=pl.CostEstimate(
            flops=4 * 2**20, bytes_accessed=20 * 2**20, transcendentals=0
        ),
        name="bias",
    )(edges, low, high)


def layer_norm(values, gain, offset):
    centre = jnp.mean(values, axis=-1, keepdims=True)
    centred = values - centre
    spread = jnp.mean(centred * centred, axis=-1, keepdims=True)
    return centred * lax.rsqrt(spread + 1e-05) * gain + offset


def gelu(x):
    return 0.5 * x * (1.0 + lax.erf(x * jnp.float32(math.sqrt(0.5))))


def window_kernel(
    first,
    tissue_ref,
    scale_ref,
    top_ref,
    bottom_ref,
    wqkv_ref,
    wproj_ref,
    wfc1_ref,
    wfc2_ref,
    norm_ref,
    bias_ref,
    top_out_ref,
    bottom_out_ref,
    triple_ref,
    mixed_ref,
    raised_ref,
):
    w = pl.program_id(0)
    half = SHIFT * WIN
    x = jnp.concatenate(
        [top_ref[...].reshape(half, DIM), bottom_ref[...].reshape(half, DIM)], axis=0
    )
    triple = nt_dot(wqkv_ref[...], x).astype(jnp.bfloat16)
    for at in range(2):
        part = triple[at * DIM : (at + 1) * DIM].astype(jnp.float32)
        part = part.reshape(HEADS, HEAD_DIM, TOKENS)
        part = part * lax.rsqrt(jnp.sum(part * part, axis=1, keepdims=True) + 1e-06)
        triple_ref[at * DIM : (at + 1) * DIM, :] = part.reshape(DIM, TOKENS).astype(jnp.bfloat16)
    triple_ref[2 * DIM :, :] = triple[2 * DIM :]
    ones = jnp.ones((16, TOKENS), jnp.bfloat16)
    def score(h):
        at = h * HEAD_DIM
        query = triple_ref[at : at + HEAD_DIM, :]
        key = triple_ref[DIM + at : DIM + at + HEAD_DIM, :]
        return tn_dot(key, query) * scale_ref[h] + bias_ref[h]

    def soften(scores):
        highest = jnp.max(scores, axis=0, keepdims=True)
        return jnp.exp2(scores - highest).astype(jnp.bfloat16)

    def mix(h, raised):
        at = h * HEAD_DIM
        value = triple_ref[2 * DIM + at : 2 * DIM + at + HEAD_DIM, :]
        both = nn_dot(jnp.concatenate([value, ones], axis=0), raised)
        mixed = both[:HEAD_DIM] * (1.0 / both[HEAD_DIM : HEAD_DIM + 1])
        mixed_ref[at : at + HEAD_DIM, :] = mixed.astype(jnp.bfloat16)

    for h in range(HEADS):
        raised_ref[h] = soften(score(h))
    for h in range(HEADS):
        mix(h, raised_ref[h])
    keep = tissue_ref[0, first + w].astype(jnp.float32)
    projected = tn_dot(mixed_ref[...], wproj_ref[...])
    branch = layer_norm(projected, norm_ref[0:1, :], norm_ref[1:2, :])
    after = (x.astype(jnp.float32) + keep * branch).astype(jnp.bfloat16)
    hidden = gelu(nn_dot(after, wfc1_ref[...])).astype(jnp.bfloat16)
    grown = nn_dot(hidden, wfc2_ref[...])
    branch = layer_norm(grown, norm_ref[2:3, :], norm_ref[3:4, :])
    final = (after.astype(jnp.float32) + keep * branch).astype(jnp.bfloat16)
    top_out_ref[...] = final[:half].reshape(SHIFT, WIN, DIM)
    bottom_out_ref[...] = final[half:].reshape(SHIFT, WIN, DIM)


def run_windows(tissue, scale, weights, norms, first, top, bottom, bias):
    count = top.shape[1] // WIN
    smem = pl.BlockSpec(memory_space=pltpu.SMEM)
    whole = pl.BlockSpec(memory_space=pltpu.VMEM)
    tile = pl.BlockSpec((SHIFT, WIN, DIM), lambda w: (0, w, 0))
    half = jax.ShapeDtypeStruct(top.shape, jnp.bfloat16)
    return pl.pallas_call(
        functools.partial(window_kernel, first),
        grid=(count,),
        out_shape=[half, half],
        in_specs=[smem, smem, tile, tile] + [whole] * 6,
        out_specs=[tile, tile],
        scratch_shapes=[
            pltpu.VMEM((3 * DIM, TOKENS), jnp.bfloat16),
            pltpu.VMEM((DIM, TOKENS), jnp.bfloat16),
            pltpu.VMEM((HEADS, TOKENS, TOKENS), jnp.bfloat16),
        ],
        compiler_params=pltpu.CompilerParams(
            vmem_limit_bytes=32 * 2**20, dimension_semantics=("arbitrary",)
        ),
        cost_estimate=pl.CostEstimate(
            flops=count * 7 * 10**9, bytes_accessed=4 * 2**20, transcendentals=count * 2**20
        ),
        name="windows",
    )(tissue, scale, top, bottom, *weights, norms, bias)


def on_device(
    crop,
    tissue,
    w_qkv,
    w_proj,
    w_fc1,
    w_fc2,
    logit_scale,
    bias_table,
    norm1_gain,
    norm1_bias,
    norm2_gain,
    norm2_bias,
):
    tile_cols = crop.shape[1]
    edges = jnp.stack(
        [
            (lax.axis_index("row") == lax.axis_size("row") - 1).astype(jnp.int32),
            (lax.axis_index("col") == lax.axis_size("col") - 1).astype(jnp.int32),
        ]
    )
    scale = jnp.exp(jnp.minimum(logit_scale, math.log(100.0))) * jnp.float32(LOG2E)
    weights = (w_qkv.T, w_proj, w_fc1, w_fc2)
    norms = jnp.stack([norm1_gain, norm1_bias, norm2_gain, norm2_bias])
    inner_bias, last_bias = build_bias(edges, bias_table)
    windows = tile_cols // WIN
    middle = windows // 2 * WIN
    right = tile_cols - WIN
    side = shifted(crop[SHIFT:, :SHIFT], "col", -1)
    corner = shifted_both(crop[:SHIFT, :SHIFT], -1)
    split = middle + SHIFT
    below_right = shifted(crop[:SHIFT, split:], "row", -1)
    below_left = shifted(crop[:SHIFT, SHIFT:split], "row", -1)
    run = functools.partial(run_windows, tissue, scale, weights, norms)
    end = right + SHIFT - split
    top_end, bottom_end = run(
        windows - 1,
        jnp.concatenate([crop[SHIFT:, right + SHIFT :], side], axis=1),
        jnp.concatenate([below_right[:, end:], corner], axis=1),
        last_bias,
    )
    from_left = shifted(top_end[:, SHIFT:], "col", 1)
    from_corner = shifted_both(bottom_end[:, SHIFT:], 1)
    top_right, bottom_right = run(
        windows // 2, crop[SHIFT:, split : right + SHIFT], below_right[:, :end], inner_bias
    )
    above_right = shifted(
        jnp.concatenate([bottom_right, bottom_end[:, :SHIFT]], axis=1), "row", 1
    )
    top_left, bottom_left = run(0, crop[SHIFT:, SHIFT:split], below_left, inner_bias)
    above_left = shifted(bottom_left, "row", 1)
    upper = jnp.concatenate([from_corner, above_left, above_right], axis=1)
    lower = jnp.concatenate([from_left, top_left, top_right, top_end[:, :SHIFT]], axis=1)
    return jnp.concatenate([upper, lower], axis=0)


def solution(mesh):
    in_specs = (P("row", "col", None), P("row", "col")) + (P(),) * 10
    return jax.shard_map(
        on_device,
        mesh=mesh,
        in_specs=in_specs,
        out_specs=P("row", "col", None),
        check_vma=False,
    )
```

```python
import functools
import math

import jax
import jax.numpy as jnp
from jax import lax
from jax.experimental import pallas as pl
from jax.experimental.pallas import tpu as pltpu
from jax.sharding import PartitionSpec as P

DIM = 512
HEADS = 16
WIN = 16
HEAD_DIM = 32
SHIFT = 8
TOKENS = WIN * WIN
SPAN = 2 * WIN * WIN
LOG2E = math.log2(math.e)


def shifted(x, axis, by):
    count = lax.axis_size(axis)
    return lax.ppermute(x, axis, [(i, (i + by) % count) for i in range(count)])


def shifted_both(x, by):
    rows, cols = (lax.axis_size("row"), lax.axis_size("col"))
    pairs = [
        (r * cols + c, (r + by) % rows * cols + (c + by) % cols)
        for r in range(rows)
        for c in range(cols)
    ]
    return lax.ppermute(x, ("row", "col"), pairs)


def nt_dot(a, b):
    return lax.dot_general(a, b, (((1,), (1,)), ((), ())), preferred_element_type=jnp.float32)


def tn_dot(a, b):
    return lax.dot_general(a, b, (((0,), (0,)), ((), ())), preferred_element_type=jnp.float32)


def nn_dot(a, b):
    return lax.dot_general(a, b, (((1,), (0,)), ((), ())), preferred_element_type=jnp.float32)


def half_of(axis):
    key = lax.broadcasted_iota(jnp.int32, (TOKENS, TOKENS), 0)
    query = lax.broadcasted_iota(jnp.int32, (TOKENS, TOKENS), 1)
    if axis == 0:
        key, query = key // WIN, query // WIN
    else:
        key, query = key % WIN, query % WIN
    return (key < SHIFT) != (query < SHIFT)


def bias_kernel(edge_ref, low_ref, high_ref, inner_ref, last_ref, rows_ref, pen_ref):
    low = low_ref[...]
    high = high_ref[...]
    place = lax.broadcasted_iota(jnp.int32, (HEADS, SPAN), 1) % WIN
    for y in range(WIN):
        s = WIN - 1 - y
        first = pltpu.roll(low, (SPAN - s) % SPAN, 1)
        second = pltpu.roll(high, WIN - s, 1)
        rows_ref[:, y, :] = jnp.where(place < WIN - s, first, second)
    by_row = half_of(0) & (edge_ref[0] == 1)
    by_col = half_of(1) & (edge_ref[1] == 1)
    row_pen = jnp.where(by_row, jnp.float32(-100.0 * LOG2E), jnp.float32(0.0))
    pen_ref[0] = row_pen
    pen_ref[1] = jnp.where(by_col, jnp.float32(-100.0 * LOG2E), row_pen)

    def one_head(h, carry):
        rows = rows_ref[h]
        for v in range(WIN):
            lanes = WIN * (WIN - 1 - v)
            moved = pltpu.roll(rows, (SPAN - lanes) % SPAN, 1)[:, :TOKENS]
            at = slice(v * WIN, (v + 1) * WIN)
            inner_ref[h, at, :] = moved + pen_ref[0, at, :]
            last_ref[h, at, :] = moved + pen_ref[1, at, :]
        return carry

    lax.fori_loop(0, HEADS, one_head, 0)


def build_bias(edges, bias_table):
    table = jnp.pad(bias_table * jnp.float32(LOG2E), ((0, 0), (0, 1), (0, 1)))
    low = table[:, :, :WIN].reshape(HEADS, SPAN)
    high = table[:, :, WIN:].reshape(HEADS, SPAN)
    return pl.pallas_call(
        bias_kernel,
        out_shape=[jax.ShapeDtypeStruct((HEADS, TOKENS, TOKENS), jnp.float32)] * 2,
        in_specs=[
            pl.BlockSpec(memory_space=pltpu.SMEM),
            pl.BlockSpec(memory_space=pltpu.VMEM),
            pl.BlockSpec(memory_space=pltpu.VMEM),
        ],
        out_specs=[pl.BlockSpec(memory_space=pltpu.VMEM)] * 2,
        scratch_shapes=[
            pltpu.VMEM((HEADS, WIN, SPAN), jnp.float32),
            pltpu.VMEM((2, TOKENS, TOKENS), jnp.float32),
        ],
        compiler_params=pltpu.CompilerParams(vmem_limit_bytes=24 * 2**20),
        cost_estimate=pl.CostEstimate(
            flops=4 * 2**20, bytes_accessed=20 * 2**20, transcendentals=0
        ),
        name="bias",
    )(edges, low, high)


def layer_norm(values, gain, offset):
    centre = jnp.mean(values, axis=-1, keepdims=True)
    centred = values - centre
    spread = jnp.mean(centred * centred, axis=-1, keepdims=True)
    return centred * lax.rsqrt(spread + 1e-05) * gain + offset


def gelu(x):
    return 0.5 * x * (1.0 + lax.erf(x * jnp.float32(math.sqrt(0.5))))


def window_kernel(
    first,
    unused,
    tissue_ref,
    scale_ref,
    top_ref,
    bottom_ref,
    wqkv_ref,
    wproj_ref,
    wfc1_ref,
    wfc2_ref,
    norm_ref,
    bias_ref,
    *refs,
):
    top_out_ref, bottom_out_ref, triple_ref, mixed_ref, raised_ref = refs[unused:]
    w = pl.program_id(0)
    half = SHIFT * WIN
    x = jnp.concatenate(
        [top_ref[...].reshape(half, DIM), bottom_ref[...].reshape(half, DIM)], axis=0
    )
    triple = nt_dot(wqkv_ref[...], x).astype(jnp.bfloat16)
    for at in range(2):
        part = triple[at * DIM : (at + 1) * DIM].astype(jnp.float32)
        part = part.reshape(HEADS, HEAD_DIM, TOKENS)
        part = part * lax.rsqrt(jnp.sum(part * part, axis=1, keepdims=True) + 1e-06)
        triple_ref[at * DIM : (at + 1) * DIM, :] = part.reshape(DIM, TOKENS).astype(jnp.bfloat16)
    triple_ref[2 * DIM :, :] = triple[2 * DIM :]
    ones = jnp.ones((16, TOKENS), jnp.bfloat16)
    def score(h):
        at = h * HEAD_DIM
        query = triple_ref[at : at + HEAD_DIM, :]
        key = triple_ref[DIM + at : DIM + at + HEAD_DIM, :]
        return tn_dot(key, query) * scale_ref[h] + bias_ref[h]

    def soften(scores):
        highest = jnp.max(scores, axis=0, keepdims=True)
        return jnp.exp2(scores - highest).astype(jnp.bfloat16)

    def mix(h, raised):
        at = h * HEAD_DIM
        value = triple_ref[2 * DIM + at : 2 * DIM + at + HEAD_DIM, :]
        both = nn_dot(jnp.concatenate([value, ones], axis=0), raised)
        mixed = both[:HEAD_DIM] * (1.0 / both[HEAD_DIM : HEAD_DIM + 1])
        mixed_ref[at : at + HEAD_DIM, :] = mixed.astype(jnp.bfloat16)

    for h in range(HEADS):
        raised_ref[h] = soften(score(h))
    for h in range(HEADS):
        mix(h, raised_ref[h])
    keep = tissue_ref[0, first + w].astype(jnp.float32)
    projected = tn_dot(mixed_ref[...], wproj_ref[...])
    branch = layer_norm(projected, norm_ref[0:1, :], norm_ref[1:2, :])
    after = (x.astype(jnp.float32) + keep * branch).astype(jnp.bfloat16)
    hidden = gelu(nn_dot(after, wfc1_ref[...])).astype(jnp.bfloat16)
    grown = nn_dot(hidden, wfc2_ref[...])
    branch = layer_norm(grown, norm_ref[2:3, :], norm_ref[3:4, :])
    final = (after.astype(jnp.float32) + keep * branch).astype(jnp.bfloat16)
    top_out_ref[...] = final[:half].reshape(SHIFT, WIN, DIM)
    bottom_out_ref[...] = final[half:].reshape(SHIFT, WIN, DIM)


def run_windows(tissue, scale, weights, norms, first, top, bottom, bias, after=()):
    count = top.shape[1] // WIN
    smem = pl.BlockSpec(memory_space=pltpu.SMEM)
    whole = pl.BlockSpec(memory_space=pltpu.VMEM)
    tile = pl.BlockSpec((SHIFT, WIN, DIM), lambda w: (0, w, 0))
    half = jax.ShapeDtypeStruct(top.shape, jnp.bfloat16)
    return pl.pallas_call(
        functools.partial(window_kernel, first, len(after)),
        grid=(count,),
        out_shape=[half, half],
        in_specs=[smem, smem, tile, tile]
        + [whole] * 6
        + [pl.BlockSpec(memory_space=pl.ANY)] * len(after),
        out_specs=[tile, tile],
        scratch_shapes=[
            pltpu.VMEM((3 * DIM, TOKENS), jnp.bfloat16),
            pltpu.VMEM((DIM, TOKENS), jnp.bfloat16),
            pltpu.VMEM((HEADS, TOKENS, TOKENS), jnp.bfloat16),
        ],
        compiler_params=pltpu.CompilerParams(
            vmem_limit_bytes=32 * 2**20, dimension_semantics=("arbitrary",)
        ),
        cost_estimate=pl.CostEstimate(
            flops=count * 7 * 10**9, bytes_accessed=4 * 2**20, transcendentals=count * 2**20
        ),
        name="windows",
    )(tissue, scale, top, bottom, *weights, norms, bias, *after)


def on_device(
    crop,
    tissue,
    w_qkv,
    w_proj,
    w_fc1,
    w_fc2,
    logit_scale,
    bias_table,
    norm1_gain,
    norm1_bias,
    norm2_gain,
    norm2_bias,
):
    tile_cols = crop.shape[1]
    edges = jnp.stack(
        [
            (lax.axis_index("row") == lax.axis_size("row") - 1).astype(jnp.int32),
            (lax.axis_index("col") == lax.axis_size("col") - 1).astype(jnp.int32),
        ]
    )
    scale = jnp.exp(jnp.minimum(logit_scale, math.log(100.0))) * jnp.float32(LOG2E)
    weights = (w_qkv.T, w_proj, w_fc1, w_fc2)
    norms = jnp.stack([norm1_gain, norm1_bias, norm2_gain, norm2_bias])
    inner_bias, last_bias = build_bias(edges, bias_table)
    windows = tile_cols // WIN
    middle = windows // 2 * WIN
    right = tile_cols - WIN
    side = shifted(crop[SHIFT:, :SHIFT], "col", -1)
    corner = shifted_both(crop[:SHIFT, :SHIFT], -1)
    split = middle + SHIFT
    below_right = shifted(crop[:SHIFT, split:], "row", -1)
    below_left = shifted(crop[:SHIFT, SHIFT:split], "row", -1)
    run = functools.partial(run_windows, tissue, scale, weights, norms)
    end = right + SHIFT - split
    top_end, bottom_end = run(
        windows - 1,
        jnp.concatenate([crop[SHIFT:, right + SHIFT :], side], axis=1),
        jnp.concatenate([below_right[:, end:], corner], axis=1),
        last_bias,
    )
    from_left = shifted(top_end[:, SHIFT:], "col", 1)
    from_corner = shifted_both(bottom_end[:, SHIFT:], 1)
    top_right, bottom_right = run(
        windows // 2, crop[SHIFT:, split : right + SHIFT], below_right[:, :end], inner_bias
    )
    above_right = shifted(
        jnp.concatenate([bottom_right, bottom_end[:, :SHIFT]], axis=1), "row", 1
    )
    cuts = [windows // 2, windows // 4, windows // 8, 0]
    sent = [(above_right, from_left, from_corner)]
    own, above = ([top_right, top_end[:, :SHIFT]], [above_right])
    for step, (hi, lo) in enumerate(zip(cuts, cuts[1:])):
        start, stop = (lo * WIN, hi * WIN)
        top, bottom = run(
            lo,
            crop[SHIFT:, start + SHIFT : stop + SHIFT],
            below_left[:, start:stop],
            inner_bias,
            sent[step - 1] + (own[0],) if step >= 1 else (),
        )
        own.insert(0, top)
        above.insert(0, shifted(bottom, "row", 1))
        sent.append((above[0],))
    upper = jnp.concatenate([from_corner] + above, axis=1)
    lower = jnp.concatenate([from_left] + own, axis=1)
    return jnp.concatenate([upper, lower], axis=0)


def solution(mesh):
    in_specs = (P("row", "col", None), P("row", "col")) + (P(),) * 10
    return jax.shard_map(
        on_device,
        mesh=mesh,
        in_specs=in_specs,
        out_specs=P("row", "col", None),
        check_vma=False,
    )
```

```python
import functools
import math

import jax
import jax.numpy as jnp
from jax import lax
from jax.experimental import pallas as pl
from jax.experimental.pallas import tpu as pltpu
from jax.sharding import PartitionSpec as P

DIM = 512
HEADS = 16
WIN = 16
HEAD_DIM = 32
SHIFT = 8
TOKENS = WIN * WIN
SPAN = 2 * WIN * WIN
LOG2E = math.log2(math.e)


def shifted(x, axis, by):
    count = lax.axis_size(axis)
    return lax.ppermute(x, axis, [(i, (i + by) % count) for i in range(count)])


def shifted_both(x, by):
    rows, cols = (lax.axis_size("row"), lax.axis_size("col"))
    pairs = [
        (r * cols + c, (r + by) % rows * cols + (c + by) % cols)
        for r in range(rows)
        for c in range(cols)
    ]
    return lax.ppermute(x, ("row", "col"), pairs)


def nt_dot(a, b):
    return lax.dot_general(a, b, (((1,), (1,)), ((), ())), preferred_element_type=jnp.float32)


def tn_dot(a, b):
    return lax.dot_general(a, b, (((0,), (0,)), ((), ())), preferred_element_type=jnp.float32)


def nn_dot(a, b):
    return lax.dot_general(a, b, (((1,), (0,)), ((), ())), preferred_element_type=jnp.float32)


def half_of(axis):
    key = lax.broadcasted_iota(jnp.int32, (TOKENS, TOKENS), 0)
    query = lax.broadcasted_iota(jnp.int32, (TOKENS, TOKENS), 1)
    if axis == 0:
        key, query = key // WIN, query // WIN
    else:
        key, query = key % WIN, query % WIN
    return (key < SHIFT) != (query < SHIFT)


def bias_kernel(edge_ref, low_ref, high_ref, inner_ref, last_ref, rows_ref, pen_ref):
    low = low_ref[...]
    high = high_ref[...]
    place = lax.broadcasted_iota(jnp.int32, (HEADS, SPAN), 1) % WIN
    for y in range(WIN):
        s = WIN - 1 - y
        first = pltpu.roll(low, (SPAN - s) % SPAN, 1)
        second = pltpu.roll(high, WIN - s, 1)
        rows_ref[:, y, :] = jnp.where(place < WIN - s, first, second)
    by_row = half_of(0) & (edge_ref[0] == 1)
    by_col = half_of(1) & (edge_ref[1] == 1)
    row_pen = jnp.where(by_row, jnp.float32(-100.0 * LOG2E), jnp.float32(0.0))
    pen_ref[0] = row_pen
    pen_ref[1] = jnp.where(by_col, jnp.float32(-100.0 * LOG2E), row_pen)

    def one_head(h, carry):
        rows = rows_ref[h]
        for v in range(WIN):
            lanes = WIN * (WIN - 1 - v)
            moved = pltpu.roll(rows, (SPAN - lanes) % SPAN, 1)[:, :TOKENS]
            at = slice(v * WIN, (v + 1) * WIN)
            inner_ref[h, at, :] = moved + pen_ref[0, at, :]
            last_ref[h, at, :] = moved + pen_ref[1, at, :]
        return carry

    lax.fori_loop(0, HEADS, one_head, 0)


def build_bias(edges, bias_table):
    table = jnp.pad(bias_table * jnp.float32(LOG2E), ((0, 0), (0, 1), (0, 1)))
    low = table[:, :, :WIN].reshape(HEADS, SPAN)
    high = table[:, :, WIN:].reshape(HEADS, SPAN)
    return pl.pallas_call(
        bias_kernel,
        out_shape=[jax.ShapeDtypeStruct((HEADS, TOKENS, TOKENS), jnp.float32)] * 2,
        in_specs=[
            pl.BlockSpec(memory_space=pltpu.SMEM),
            pl.BlockSpec(memory_space=pltpu.VMEM),
            pl.BlockSpec(memory_space=pltpu.VMEM),
        ],
        out_specs=[pl.BlockSpec(memory_space=pltpu.VMEM)] * 2,
        scratch_shapes=[
            pltpu.VMEM((HEADS, WIN, SPAN), jnp.float32),
            pltpu.VMEM((2, TOKENS, TOKENS), jnp.float32),
        ],
        compiler_params=pltpu.CompilerParams(vmem_limit_bytes=24 * 2**20),
        cost_estimate=pl.CostEstimate(
            flops=4 * 2**20, bytes_accessed=20 * 2**20, transcendentals=0
        ),
        name="bias",
    )(edges, low, high)


def layer_norm(values, gain, offset):
    centre = jnp.mean(values, axis=-1, keepdims=True)
    centred = values - centre
    spread = jnp.mean(centred * centred, axis=-1, keepdims=True)
    return centred * lax.rsqrt(spread + 1e-05) * gain + offset


def gelu(x):
    return 0.5 * x * (1.0 + lax.erf(x * jnp.float32(math.sqrt(0.5))))


def window_kernel(
    first,
    unused,
    tissue_ref,
    scale_ref,
    top_ref,
    bottom_ref,
    wqkv_ref,
    wproj_ref,
    wfc1_ref,
    wfc2_ref,
    norm_ref,
    bias_ref,
    *refs,
):
    top_out_ref, bottom_out_ref, triple_ref, mixed_ref, raised_ref = refs[unused:]
    w = pl.program_id(0)
    half = SHIFT * WIN
    x = jnp.concatenate(
        [top_ref[...].reshape(half, DIM), bottom_ref[...].reshape(half, DIM)], axis=0
    )
    triple = nt_dot(wqkv_ref[...], x).astype(jnp.bfloat16)
    for at in range(2):
        part = triple[at * DIM : (at + 1) * DIM].astype(jnp.float32)
        part = part.reshape(HEADS, HEAD_DIM, TOKENS)
        part = part * lax.rsqrt(jnp.sum(part * part, axis=1, keepdims=True) + 1e-06)
        triple_ref[at * DIM : (at + 1) * DIM, :] = part.reshape(DIM, TOKENS).astype(jnp.bfloat16)
    triple_ref[2 * DIM :, :] = triple[2 * DIM :]
    ones = jnp.ones((16, TOKENS), jnp.bfloat16)
    def score(h):
        at = h * HEAD_DIM
        query = triple_ref[at : at + HEAD_DIM, :]
        key = triple_ref[DIM + at : DIM + at + HEAD_DIM, :]
        return tn_dot(key, query) * scale_ref[h] + bias_ref[h]

    def soften(scores):
        highest = jnp.max(scores, axis=0, keepdims=True)
        return jnp.exp2(scores - highest).astype(jnp.bfloat16)

    def mix(h, raised):
        at = h * HEAD_DIM
        value = triple_ref[2 * DIM + at : 2 * DIM + at + HEAD_DIM, :]
        both = nn_dot(jnp.concatenate([value, ones], axis=0), raised)
        mixed = both[:HEAD_DIM] * (1.0 / both[HEAD_DIM : HEAD_DIM + 1])
        mixed_ref[at : at + HEAD_DIM, :] = mixed.astype(jnp.bfloat16)

    for h in range(HEADS):
        raised_ref[h] = soften(score(h))
    for h in range(HEADS):
        mix(h, raised_ref[h])
    keep = tissue_ref[0, first + w].astype(jnp.float32)
    projected = tn_dot(mixed_ref[...], wproj_ref[...])
    branch = layer_norm(projected, norm_ref[0:1, :], norm_ref[1:2, :])
    after = (x.astype(jnp.float32) + keep * branch).astype(jnp.bfloat16)
    hidden = gelu(nn_dot(after, wfc1_ref[...])).astype(jnp.bfloat16)
    grown = nn_dot(hidden, wfc2_ref[...])
    branch = layer_norm(grown, norm_ref[2:3, :], norm_ref[3:4, :])
    final = (after.astype(jnp.float32) + keep * branch).astype(jnp.bfloat16)
    top_out_ref[...] = final[:half].reshape(SHIFT, WIN, DIM)
    bottom_out_ref[...] = final[half:].reshape(SHIFT, WIN, DIM)


def run_windows(tissue, scale, weights, norms, first, top, bottom, bias, after=()):
    count = top.shape[1] // WIN
    smem = pl.BlockSpec(memory_space=pltpu.SMEM)
    whole = pl.BlockSpec(memory_space=pltpu.VMEM)
    tile = pl.BlockSpec((SHIFT, WIN, DIM), lambda w: (0, w, 0))
    half = jax.ShapeDtypeStruct(top.shape, jnp.bfloat16)
    return pl.pallas_call(
        functools.partial(window_kernel, first, len(after)),
        grid=(count,),
        out_shape=[half, half],
        in_specs=[smem, smem, tile, tile]
        + [whole] * 6
        + [pl.BlockSpec(memory_space=pl.ANY)] * len(after),
        out_specs=[tile, tile],
        scratch_shapes=[
            pltpu.VMEM((3 * DIM, TOKENS), jnp.bfloat16),
            pltpu.VMEM((DIM, TOKENS), jnp.bfloat16),
            pltpu.VMEM((HEADS, TOKENS, TOKENS), jnp.bfloat16),
        ],
        compiler_params=pltpu.CompilerParams(
            vmem_limit_bytes=32 * 2**20, dimension_semantics=("arbitrary",)
        ),
        cost_estimate=pl.CostEstimate(
            flops=count * 7 * 10**9, bytes_accessed=4 * 2**20, transcendentals=count * 2**20
        ),
        name="windows",
    )(tissue, scale, top, bottom, *weights, norms, bias, *after)


def on_device(
    crop,
    tissue,
    w_qkv,
    w_proj,
    w_fc1,
    w_fc2,
    logit_scale,
    bias_table,
    norm1_gain,
    norm1_bias,
    norm2_gain,
    norm2_bias,
):
    tile_cols = crop.shape[1]
    edges = jnp.stack(
        [
            (lax.axis_index("row") == lax.axis_size("row") - 1).astype(jnp.int32),
            (lax.axis_index("col") == lax.axis_size("col") - 1).astype(jnp.int32),
        ]
    )
    scale = jnp.exp(jnp.minimum(logit_scale, math.log(100.0))) * jnp.float32(LOG2E)
    weights = (w_qkv.T, w_proj, w_fc1, w_fc2)
    norms = jnp.stack([norm1_gain, norm1_bias, norm2_gain, norm2_bias])
    inner_bias, last_bias = build_bias(edges, bias_table)
    windows = tile_cols // WIN
    middle = windows // 2 * WIN
    right = tile_cols - WIN
    side = shifted(crop[SHIFT:, :SHIFT], "col", -1)
    corner = shifted_both(crop[:SHIFT, :SHIFT], -1)
    split = middle + SHIFT
    below_right = shifted(crop[:SHIFT, split:], "row", -1)
    below_left = shifted(crop[:SHIFT, SHIFT:split], "row", -1)
    run = functools.partial(run_windows, tissue, scale, weights, norms)
    end = right + SHIFT - split
    top_end, bottom_end = run(
        windows - 1,
        jnp.concatenate([crop[SHIFT:, right + SHIFT :], side], axis=1),
        jnp.concatenate([below_right[:, end:], corner], axis=1),
        last_bias,
    )
    from_left = shifted(top_end[:, SHIFT:], "col", 1)
    from_corner = shifted_both(bottom_end[:, SHIFT:], 1)
    top_right, bottom_right = run(
        windows // 2, crop[SHIFT:, split : right + SHIFT], below_right[:, :end], inner_bias
    )
    above_right = shifted(
        jnp.concatenate([bottom_right, bottom_end[:, :SHIFT]], axis=1), "row", 1
    )
    cuts = [windows // 2, windows // 4, 0]
    sent = [(above_right, from_left, from_corner)]
    own, above = ([top_right, top_end[:, :SHIFT]], [above_right])
    for step, (hi, lo) in enumerate(zip(cuts, cuts[1:])):
        start, stop = (lo * WIN, hi * WIN)
        top, bottom = run(
            lo,
            crop[SHIFT:, start + SHIFT : stop + SHIFT],
            below_left[:, start:stop],
            inner_bias,
            sent[step - 1] + (own[0],) if step >= 1 else (),
        )
        own.insert(0, top)
        above.insert(0, shifted(bottom, "row", 1))
        sent.append((above[0],))
    upper = jnp.concatenate([from_corner] + above, axis=1)
    lower = jnp.concatenate([from_left] + own, axis=1)
    return jnp.concatenate([upper, lower], axis=0)


def solution(mesh):
    in_specs = (P("row", "col", None), P("row", "col")) + (P(),) * 10
    return jax.shard_map(
        on_device,
        mesh=mesh,
        in_specs=in_specs,
        out_specs=P("row", "col", None),
        check_vma=False,
    )
```
